32 devices in a mesh: dp: 4 (over y, core), mp: 8 (over z, x).
Axes of the slice: x: 2, y: 2, z: 4, core: 2. Of those that a mesh axis runs over, the one named last changes fastest.
Arguments:
- tokens: bfloat16 [512, 8192], P('dp', 'mp'), may hold values from -6 to 6
- cotangent: bfloat16 [512, 28672], P('dp', 'mp'), may hold values from -2 to 2
- tiles: bfloat16 [2, 1344, 128, 128], P(None, 'mp'), may hold values from -0.1875 to 0.1875
- tile_rows: int32 [2, 1344], replicated, may hold values from 0 to 63, as said below
- tile_cols: int32 [2, 1344], replicated, may hold values from 0 to 223, as said below
Outputs:
- hidden: bfloat16 [512, 28672], P('dp', 'mp')
- input_grad: bfloat16 [512, 8192], P('dp', 'mp')
- tile_grads: float32 [2, 1344, 128, 128], P(None, 'mp')
The draws below stay inside these ranges and needn't reach their ends.
Inputs may be any that keep to these rules, and one draw needn't show every extreme that they name: `tile_rows`: row m lists the tiles of matrix m; device k // 168 of mp owns tile k. Within one column panel of one matrix the row blocks are distinct. `tile_cols`: A column panel holds 12 or 4 tiles, the same count for all 28 panels of one holder (panels c with equal c // 28), 12 for a quarter of the holders. An owner's tiles are listed in the order of their panels. At most 42 of one owner's tiles of a matrix lie in one holder's panels, and this bound is reached in every matrix.
All inputs are finite; a program needn't handle non-finite values.
Results may differ from the reference program's by a relative error of at most 0.02.
Values may be sent and summed in bfloat16 or wider, within the bound.
A program may use at most 192 MiB of HBM per device.

```python
import jax
import jax.numpy as jnp
from jax import lax

D = 8192
FF = 28672
BLOCK = 128
KHEAVY = 12
KLIGHT = 4
GTOK = 128
RB = 64
CB = 224
NT = 1344
TOKENS = 512
N_DP = 4
N_MP = 8


def mask_layout(key, matrix):
    key = jax.random.fold_in(key, 100 + matrix)
    holder_key, order_key, owner_key = jax.random.split(key, 3)
    panel_count = FF // BLOCK
    per_holder = panel_count // N_MP
    owned_count = per_holder * (KHEAVY + 3 * KLIGHT) // 4
    listed = owned_count * N_MP
    holder_rank = jax.random.permutation(holder_key, N_MP)
    heavy = holder_rank < N_MP // 4
    counts = jnp.where(heavy[jnp.arange(panel_count) // per_holder], KHEAVY, KLIGHT).astype(jnp.int32)
    ends = jnp.cumsum(counts)
    position = jnp.arange(listed, dtype=jnp.int32)
    column = jnp.sum((ends[None, :] <= position[:, None]).astype(jnp.int32), axis=1)
    within = position - (ends[column] - counts[column])
    orders = jax.vmap(lambda sub_key: jax.random.permutation(sub_key, D // BLOCK))(jax.random.split(order_key, panel_count))
    row = orders[column, within].astype(jnp.int32)
    owner_perm = jax.random.permutation(owner_key, N_MP)
    residue = jnp.argsort(owner_perm).astype(jnp.int32)
    layout = (residue[:, None] + N_MP * jnp.arange(owned_count, dtype=jnp.int32)[None, :]).reshape(-1)
    return (row[layout], column[layout])


def draw_tile_rows(key, part):
    shared = [mask_layout(key, matrix) for matrix in range(2)]
    return jnp.stack([shared[0][0], shared[1][0]]).astype(jnp.int32)


def draw_tile_cols(key, part):
    shared = [mask_layout(key, matrix) for matrix in range(2)]
    return jnp.stack([shared[0][1], shared[1][1]]).astype(jnp.int32)


def level_of(own_key, extent, cuts, least, top_value):
    level = 1.0
    for dim, parts in cuts:
        steps = jax.random.uniform(jax.random.fold_in(jax.random.fold_in(own_key, 6), dim), (parts,), jnp.float32, least / len(cuts), top_value / len(cuts))
        level = level * jnp.repeat(jnp.exp(steps), extent[dim] // parts).reshape((-1,) + (1,) * (len(extent) - 1 - dim))
    return level


def gaussian(own_key, extent, scale, most, cuts=(), held_as=jnp.bfloat16):
    level = level_of(own_key, extent, cuts, -0.22, 0.18) if cuts else 1.0
    values = jax.random.normal(own_key, extent, jnp.float32) * scale * level
    return jnp.minimum(jnp.maximum(values, -most), most).astype(held_as)


def setup_inputs(seed: int = 0) -> dict:
    key_list = jax.random.split(jax.random.key(seed), 6)
    tokens = gaussian(key_list[0], (TOKENS, D), 1.0, 6.0, ((0, 4), (1, 8)))
    cotangent = gaussian(key_list[1], (TOKENS, FF), 0.25, 2.0, ((0, 4), (1, 8)))
    tiles = gaussian(key_list[2], (2, NT, BLOCK, BLOCK), (8 * BLOCK) ** -0.5, 0.1875, ((1, 8),))
    tile_rows = draw_tile_rows(jax.random.fold_in(key_list[5], 71), 0)
    tile_cols = draw_tile_cols(jax.random.fold_in(key_list[5], 71), 0)
    return dict(tokens=tokens, cotangent=cotangent, tiles=tiles, tile_rows=tile_rows, tile_cols=tile_cols)


def reference(tokens, cotangent, tiles, tile_rows, tile_cols):
    weights = tiles.astype(jnp.float32)
    grad_total = jnp.zeros((2, NT, BLOCK, BLOCK), jnp.float32)
    hidden_parts = []
    input_parts = []
    for group_index in range(N_DP):
        low = group_index * GTOK
        group_tokens = tokens[low:low + GTOK].astype(jnp.float32).reshape(GTOK, RB, BLOCK)
        upstream = cotangent[low:low + GTOK].astype(jnp.float32)
        projected = []
        picked = []
        for matrix in range(2):
            chosen = group_tokens[:, tile_rows[matrix]]
            partial_value = jnp.einsum("nti,tij->ntj", chosen, weights[matrix], precision=lax.Precision.HIGHEST)
            summed = jnp.zeros((GTOK, CB, BLOCK), jnp.float32).at[:, tile_cols[matrix]].add(partial_value)
            projected.append(summed.reshape(GTOK, FF))
            picked.append(chosen)
        gate_pre, up_pre = projected
        sigmoid_gate = jax.nn.sigmoid(gate_pre)
        hidden_parts.append((gate_pre * sigmoid_gate * up_pre).astype(jnp.bfloat16))
        gate_grad = (upstream * up_pre * sigmoid_gate * (1.0 + gate_pre * (1.0 - sigmoid_gate))).astype(jnp.bfloat16)
        up_grad = (upstream * gate_pre * sigmoid_gate).astype(jnp.bfloat16)
        input_terms = jnp.zeros((GTOK, RB, BLOCK), jnp.float32)
        for matrix, grad_panel in enumerate((gate_grad, up_grad)):
            panel_cols = grad_panel.astype(jnp.float32).reshape(GTOK, CB, BLOCK)[:, tile_cols[matrix]]
            group_grad = jnp.einsum("nti,ntj->tij", picked[matrix], panel_cols, precision=lax.Precision.HIGHEST)
            rounded = lax.optimization_barrier(group_grad.astype(jnp.bfloat16))
            grad_total = grad_total.at[matrix].add(rounded.astype(jnp.float32))
            back_terms = jnp.einsum("ntj,tij->nti", panel_cols, weights[matrix], precision=lax.Precision.HIGHEST)
            input_terms = input_terms.at[:, tile_rows[matrix]].add(back_terms)
        input_parts.append(input_terms.reshape(GTOK, D).astype(jnp.bfloat16))
    return jnp.concatenate(hidden_parts, axis=0), jnp.concatenate(input_parts, axis=0), grad_total
```

```python
import jax
import jax.numpy as jnp
from jax import lax
from jax.experimental import pallas as pl
from jax.experimental.pallas import tpu as pltpu
from jax.sharding import PartitionSpec as P

KHEAVY = 12
KLIGHT = 4
CORES = 2
VMEM_BYTES = 50 * 1024 * 1024


def load_halves(first_ref, second_ref, buf, sems):
    half = first_ref.shape[0]
    copies = [
        pltpu.make_async_copy(first_ref, buf.at[pl.ds(0, half)], sems.at[0]),
        pltpu.make_async_copy(second_ref, buf.at[pl.ds(half, half)], sems.at[1]),
    ]
    for copy in copies:
        copy.start()
    for copy in copies:
        copy.wait()


def forward_kernel(slots, rows, steps, tok_ref, first_ref, second_ref, pre_ref, buf, sems):
    load_halves(first_ref, second_ref, buf, sems)
    size = tok_ref.shape[-1]
    panels = pre_ref.shape[1] // size

    def panel_step(p, carry):
        def group(t, total):
            base = p * KHEAVY + t * KLIGHT
            left = jnp.concatenate([tok_ref[rows[base + i]] for i in range(KLIGHT)], axis=1)
            right = jnp.concatenate([buf[slots[base + i]] for i in range(KLIGHT)], axis=0)
            return total + jnp.dot(left, right, preferred_element_type=jnp.float32)

        total = lax.fori_loop(0, steps[0], group, jnp.zeros((tok_ref.shape[1], size), jnp.float32))
        pre_ref[:, pl.ds(pl.multiple_of(p * size, size), size)] = total
        return carry

    lax.fori_loop(0, panels, panel_step, 0)


def backward_kernel(
    slots, rows, steps, tokt_ref, grad_ref, first_ref, second_ref,
    terms_ref, out_first, out_second, buf, grads, sems
):
    load_halves(first_ref, second_ref, buf, sems)
    size = tokt_ref.shape[1]
    panels = grad_ref.shape[1] // size
    terms_ref[...] = jnp.zeros_like(terms_ref)

    def panel_step(p, carry):
        column = grad_ref[:, pl.ds(pl.multiple_of(p * size, size), size)]

        def group(t, inner):
            base = p * KHEAVY + t * KLIGHT
            row = [rows[base + i] for i in range(KLIGHT)]
            slot = [slots[base + i] for i in range(KLIGHT)]
            weight = jnp.concatenate([buf[s] for s in slot], axis=0)
            back = lax.dot_general(
                column, weight, (((1,), (1,)), ((), ())), preferred_element_type=jnp.float32
            )
            picked = jnp.concatenate([tokt_ref[r] for r in row], axis=0)
            outer = jnp.dot(picked, column, preferred_element_type=jnp.float32).astype(grads.dtype)
            before = [terms_ref[r] for r in row]
            for i in range(KLIGHT):
                terms_ref[row[i]] = before[i] + back[:, i * size : (i + 1) * size]
                grads[slot[i]] = outer[i * size : (i + 1) * size]
            return inner

        return lax.fori_loop(0, steps[0], group, carry)

    lax.fori_loop(0, panels, panel_step, 0)
    half = out_first.shape[0]
    copies = [
        pltpu.make_async_copy(grads.at[pl.ds(0, half)], out_first, sems.at[0]),
        pltpu.make_async_copy(grads.at[pl.ds(half, half)], out_second, sems.at[1]),
    ]
    for copy in copies:
        copy.start()
    for copy in copies:
        copy.wait()


def collect_kernel(slots, g_first, g_second, u_first, u_second, out_ref, buf, sems):
    m, c = pl.program_id(0), pl.program_id(1)

    @pl.when((m == 0) & (c == 0))
    def _():
        load_halves(g_first, g_second, buf, sems)

    @pl.when((m == 1) & (c == 0))
    def _():
        load_halves(u_first, u_second, buf, sems)

    chunk = out_ref.shape[1]
    owned = chunk * pl.num_programs(1)

    def step(i, carry):
        out_ref[0, i] = buf[slots[m * owned + c * chunk + i]].astype(jnp.float32)
        return carry

    lax.fori_loop(0, chunk, step, 0)


def per_device(tokens, cotangent, tiles, tile_rows, tile_cols):
    members = lax.axis_size("mp")
    myself = lax.axis_index("mp")
    groups = lax.axis_size("dp")
    group_id = lax.axis_index("dp")
    lanes = groups // CORES
    my_y, my_core = group_id // CORES, group_id % CORES
    size = tiles.shape[-1]
    owned = tiles.shape[1]
    tok_rows = tokens.shape[0]
    local_blocks = tokens.shape[1] // size
    row_blocks = local_blocks * members
    panels = cotangent.shape[1] // size
    capacity = (panels * KHEAVY + members - 1) // members
    share = (capacity + groups - 1) // groups
    quarter = members * share
    half = lanes * quarter
    smem = pl.BlockSpec(memory_space=pltpu.SMEM)
    vmem = pl.BlockSpec(memory_space=pltpu.VMEM)
    anywhere = pl.BlockSpec(memory_space=pl.ANY)

    def place(rank, partner):
        sender = rank % groups
        core_off = (sender % CORES + my_core) % CORES
        y_off = (my_y - sender // CORES + lanes) % lanes
        return core_off * half + y_off * quarter + partner * share + rank // groups

    def swap_cores(x):
        pairs = [(d, d - 1 if d % CORES else d + 1) for d in range(groups)]
        return lax.ppermute(x, "dp", pairs)

    def shift_y(x, by):
        pairs = [
            (d, ((d // CORES + by) % lanes) * CORES + d % CORES) for d in range(groups)
        ]
        return lax.ppermute(x, "dp", pairs)

    def spread(x):
        stacked = jnp.concatenate([x] + [shift_y(x, s) for s in range(1, lanes)], axis=0)
        return stacked, swap_cores(stacked)

    def exchange(x):
        swapped = lax.all_to_all(
            x.reshape(members, share, size, size), "mp", split_axis=0, concat_axis=0, tiled=True
        )
        return swapped.reshape(quarter, size, size)

    cols_all = tile_cols.reshape(2, members, owned)
    holder_all = cols_all // panels
    my_holder = lax.dynamic_index_in_dim(holder_all, myself, 1, keepdims=False)
    member_ids = jnp.arange(members, dtype=jnp.int32)
    tile_ids = jnp.arange(owned, dtype=jnp.int32)
    start = jnp.sum(
        (my_holder[:, None, :] < member_ids[None, :, None]).astype(jnp.int32), axis=2
    )
    source = (
        start[:, :, None] + jnp.arange(share, dtype=jnp.int32)[None, None, :] * groups + group_id
    )
    source = jnp.minimum(source, owned - 1) + jnp.arange(2, dtype=jnp.int32)[:, None, None] * owned
    flat_tiles = tiles.reshape(2 * owned, size, size)
    arrived = [
        spread(exchange(jnp.take(flat_tiles, source[m].reshape(-1), axis=0, mode="clip")))
        for m in range(2)
    ]

    blocks = jnp.transpose(tokens.reshape(tok_rows, local_blocks, size), (1, 0, 2))
    tok = lax.all_gather(blocks, "mp", axis=0, tiled=True)
    tokt = jnp.transpose(tok, (0, 2, 1))

    first = jnp.sum((holder_all < myself).astype(jnp.int32), axis=2)
    slot_all = place(
        jnp.maximum(tile_ids[None, None, :] - first[:, :, None], 0), member_ids[None, :, None]
    ).reshape(2, -1)
    local_cols = tile_cols - myself * panels
    mask = local_cols[:, None, :] == jnp.arange(panels, dtype=jnp.int32)[None, :, None]
    listed = jnp.arange(tile_cols.shape[1])
    before = (listed[:, None] < listed[None, :]).astype(jnp.bfloat16)
    rank = jnp.einsum(
        "mpk,kl->mpl", mask.astype(jnp.bfloat16), before, preferred_element_type=jnp.float32
    ).astype(jnp.int32)
    chosen = mask[:, :, None, :] & (
        rank[:, :, None, :] == jnp.arange(KHEAVY, dtype=jnp.int32)[None, None, :, None]
    )
    slots = jnp.sum(jnp.where(chosen, slot_all[:, None, None, :], 0), axis=3).reshape(2, -1)
    rows = jnp.sum(jnp.where(chosen, tile_rows[:, None, None, :], 0), axis=3).reshape(2, -1)
    steps = jnp.sum(mask[:, 0, :].astype(jnp.int32), axis=1) // KLIGHT

    slot_bytes = 2 * half * size * size * 2
    flops = 2 * panels * KHEAVY * size**2 * tok_rows
    tile_buf = pltpu.VMEM((2 * half, size, size), jnp.bfloat16)
    params = pltpu.CompilerParams(vmem_limit_bytes=VMEM_BYTES)

    def project(m):
        return pl.pallas_call(
            forward_kernel,
            out_shape=jax.ShapeDtypeStruct(cotangent.shape, jnp.float32),
            in_specs=[smem, smem, smem, vmem, anywhere, anywhere],
            out_specs=vmem,
            scratch_shapes=[tile_buf, pltpu.SemaphoreType.DMA((2,))],
            compiler_params=params,
            cost_estimate=pl.CostEstimate(
                flops=flops, bytes_accessed=4 * slot_bytes, transcendentals=0
            ),
            name="project",
        )(slots[m], rows[m], steps[m : m + 1], tok, *arrived[m])

    gate_pre, up_pre = project(0), project(1)
    sigmoid_gate = jax.nn.sigmoid(gate_pre)
    hidden = (gate_pre * sigmoid_gate * up_pre).astype(jnp.bfloat16)
    upstream = cotangent.astype(jnp.float32)
    gate_grad = (upstream * up_pre * sigmoid_gate * (1.0 + gate_pre * (1.0 - sigmoid_gate))).astype(
        jnp.bfloat16
    )
    up_grad = (upstream * gate_pre * sigmoid_gate).astype(jnp.bfloat16)

    def pull_back(m, grad):
        half_shape = jax.ShapeDtypeStruct((half, size, size), jnp.bfloat16)
        return pl.pallas_call(
            backward_kernel,
            out_shape=(
                jax.ShapeDtypeStruct((row_blocks, tok_rows, size), jnp.float32),
                half_shape,
                half_shape,
            ),
            in_specs=[smem, smem, smem, vmem, vmem, anywhere, anywhere],
            out_specs=(vmem, anywhere, anywhere),
            scratch_shapes=[tile_buf, tile_buf, pltpu.SemaphoreType.DMA((2,))],
            compiler_params=params,
            cost_estimate=pl.CostEstimate(
                flops=2 * flops, bytes_accessed=6 * slot_bytes, transcendentals=0
            ),
            name="pull_back",
        )(slots[m], rows[m], steps[m : m + 1], tokt, grad, *arrived[m])

    def total_of(kept, sent):
        wide = kept.astype(jnp.float32) + swap_cores(sent).astype(jnp.float32)
        pair = wide.astype(jnp.bfloat16).reshape(lanes, quarter, size, size)
        total = pair[0].astype(jnp.float32)
        for s in range(1, lanes):
            total = total + shift_y(pair[s], lanes - s).astype(jnp.float32)
        return spread(exchange(total.astype(jnp.bfloat16)))

    gate_terms, gate_kept, gate_sent = pull_back(0, gate_grad)
    gate_home = total_of(gate_kept, gate_sent)
    up_terms, up_kept, up_sent = pull_back(1, up_grad)
    up_home = total_of(up_kept, up_sent)

    terms = (gate_terms + up_terms).astype(jnp.bfloat16)
    mine = lax.psum_scatter(terms, "mp", scatter_dimension=0, tiled=True)
    input_grad = jnp.transpose(mine, (1, 0, 2)).reshape(tokens.shape)

    my_start = jnp.sum(
        (my_holder[:, None, :] < my_holder[:, :, None]).astype(jnp.int32), axis=2
    )
    home = place(tile_ids[None, :] - my_start, my_holder).reshape(-1)
    chunk = max(c for c in range(1, 29) if owned % c == 0)
    tile_grads = pl.pallas_call(
        collect_kernel,
        out_shape=jax.ShapeDtypeStruct(tiles.shape, jnp.float32),
        grid=(2, owned // chunk),
        in_specs=[smem, anywhere, anywhere, anywhere, anywhere],
        out_specs=pl.BlockSpec((1, chunk, size, size), lambda m, c: (m, c, 0, 0)),
        scratch_shapes=[tile_buf, pltpu.SemaphoreType.DMA((2,))],
        compiler_params=params,
        name="collect",
    )(home, *gate_home, *up_home)
    return (hidden, input_grad, tile_grads)


def solution(mesh):
    in_specs = (P("dp", "mp"), P("dp", "mp"), P(None, "mp", None, None), P(), P())
    out_specs = (P("dp", "mp"), P("dp", "mp"), P(None, "mp", None, None))
    return jax.shard_map(
        per_device, mesh=mesh, in_specs=in_specs, out_specs=out_specs, check_vma=False
    )
```

```python
import functools

import jax
import jax.numpy as jnp
from jax import lax
from jax.experimental import pallas as pl
from jax.experimental.pallas import tpu as pltpu
from jax.sharding import PartitionSpec as P

KHEAVY = 12
KLIGHT = 4
CORES = 2
VMEM_BYTES = 50 * 1024 * 1024


def load_pieces(pieces, buf, sems):
    offset = 0
    copies = []
    for i, piece in enumerate(pieces):
        count = piece.shape[0]
        copies.append(pltpu.make_async_copy(piece, buf.at[pl.ds(offset, count)], sems.at[i]))
        offset += count
    for copy in copies:
        copy.start()
    for copy in copies:
        copy.wait()


def forward_kernel(slots, rows, steps, tok_ref, *refs):
    pieces, (pre_ref, buf, sems) = refs[:-3], refs[-3:]
    load_pieces(pieces, buf, sems)
    size = tok_ref.shape[-1]
    panels = pre_ref.shape[1] // size

    def panel_step(p, carry):
        def group(t, total):
            base = p * KHEAVY + t * KLIGHT
            left = jnp.concatenate([tok_ref[rows[base + i]] for i in range(KLIGHT)], axis=1)
            right = jnp.concatenate([buf[slots[base + i]] for i in range(KLIGHT)], axis=0)
            return total + jnp.dot(left, right, preferred_element_type=jnp.float32)

        total = lax.fori_loop(0, steps[0], group, jnp.zeros((tok_ref.shape[1], size), jnp.float32))
        pre_ref[:, pl.ds(pl.multiple_of(p * size, size), size)] = total
        return carry

    lax.fori_loop(0, panels, panel_step, 0)


def backward_kernel(first, count, slots, rows, steps, tokt_ref, grad_ref, *refs):
    prior = () if first else refs[:1]
    refs = refs[len(prior) :]
    pieces, terms_out, outs = refs[:count], refs[count], refs[count + 1 : 2 * count + 1]
    buf, grads, sems = refs[2 * count + 1 : 2 * count + 4]
    terms_ref = terms_out if first else refs[-1]
    load_pieces(pieces, buf, sems)
    size = tokt_ref.shape[1]
    panels = grad_ref.shape[1] // size
    terms_ref[...] = jnp.zeros_like(terms_ref) if first else prior[0][...]

    def panel_step(p, carry):
        column = grad_ref[:, pl.ds(pl.multiple_of(p * size, size), size)]

        def group(t, inner):
            base = p * KHEAVY + t * KLIGHT
            row = [rows[base + i] for i in range(KLIGHT)]
            slot = [slots[base + i] for i in range(KLIGHT)]
            weight = jnp.concatenate([buf[s] for s in slot], axis=0)
            back = lax.dot_general(
                column, weight, (((1,), (1,)), ((), ())), preferred_element_type=jnp.float32
            )
            picked = jnp.concatenate([tokt_ref[r] for r in row], axis=0)
            outer = jnp.dot(picked, column, preferred_element_type=jnp.float32).astype(grads.dtype)
            before = [terms_ref[r] for r in row]
            for i in range(KLIGHT):
                terms_ref[row[i]] = before[i] + back[:, i * size : (i + 1) * size]
                grads[slot[i]] = outer[i * size : (i + 1) * size]
            return inner

        return lax.fori_loop(0, steps[0], group, carry)

    lax.fori_loop(0, panels, panel_step, 0)
    offset = 0
    copies = []
    for i, out in enumerate(outs):
        copies.append(
            pltpu.make_async_copy(grads.at[pl.ds(offset, out.shape[0])], out, sems.at[i])
        )
        offset += out.shape[0]
    for copy in copies:
        copy.start()
    if not first:
        terms_out[...] = terms_ref[...].astype(terms_out.dtype)
    for copy in copies:
        copy.wait()


def collect_kernel(slots, *refs):
    pieces, (out_ref, buf, sems) = refs[:-3], refs[-3:]
    m, c = pl.program_id(0), pl.program_id(1)
    each = len(pieces) // 2

    @pl.when((m == 0) & (c == 0))
    def _():
        load_pieces(pieces[:each], buf, sems)

    @pl.when((m == 1) & (c == 0))
    def _():
        load_pieces(pieces[each:], buf, sems)

    chunk = out_ref.shape[1]
    owned = chunk * pl.num_programs(1)

    def step(i, carry):
        out_ref[0, i] = buf[slots[m * owned + c * chunk + i]].astype(jnp.float32)
        return carry

    lax.fori_loop(0, chunk, step, 0, unroll=True)


def per_device(tokens, cotangent, tiles, tile_rows, tile_cols):
    members = lax.axis_size("mp")
    myself = lax.axis_index("mp")
    groups = lax.axis_size("dp")
    group_id = lax.axis_index("dp")
    lanes = groups // CORES
    my_y, my_core = group_id // CORES, group_id % CORES
    size = tiles.shape[-1]
    owned = tiles.shape[1]
    tok_rows = tokens.shape[0]
    local_blocks = tokens.shape[1] // size
    row_blocks = local_blocks * members
    panels = cotangent.shape[1] // size
    capacity = (panels * KHEAVY + members - 1) // members
    share = (capacity + groups - 1) // groups
    parts = [(0, (share + 1) // 2), ((share + 1) // 2, share // 2)]
    parts = [(low, count) for low, count in parts if count]
    packed = (owned + groups - 1) // groups
    slot_count = groups * members * share
    smem = pl.BlockSpec(memory_space=pltpu.SMEM)
    vmem = pl.BlockSpec(memory_space=pltpu.VMEM)
    anywhere = pl.BlockSpec(memory_space=pl.ANY)
    ints = jnp.int32

    def piece_of(tile):
        sender = tile % groups
        core_off = (sender % CORES + my_core) % CORES
        y_off = (my_y - sender // CORES + lanes) % lanes
        return core_off * lanes + y_off

    def skipped(start, sender):
        return (start - sender + groups - 1) // groups

    def place(piece, partner, q):
        found, base = 0, 0
        for low, count in parts:
            here = base + (piece * members + partner) * count + q - low
            found = jnp.where(q >= low, here, found)
            base += groups * members * count
        return found

    def swap_cores(x):
        pairs = [(d, d - 1 if d % CORES else d + 1) for d in range(groups)]
        return lax.ppermute(x, "dp", pairs)

    def shift_y(x, by):
        pairs = [
            (d, ((d // CORES + by) % lanes) * CORES + d % CORES) for d in range(groups)
        ]
        return lax.ppermute(x, "dp", pairs)

    def spread(x):
        mine = [x] + [shift_y(x, s) for s in range(1, lanes)]
        return mine + [swap_cores(piece) for piece in mine]

    def exchange(x):
        swapped = lax.all_to_all(
            x.reshape(members, -1, size, size), "mp", split_axis=0, concat_axis=0, tiled=True
        )
        return swapped.reshape(-1, size, size)

    cols_all = tile_cols.reshape(2, members, owned)
    holder_all = cols_all // panels
    my_holder = lax.dynamic_index_in_dim(holder_all, myself, 1, keepdims=False)
    member_ids = jnp.arange(members, dtype=ints)
    tile_ids = jnp.arange(owned, dtype=ints)
    start = jnp.sum((my_holder[:, None, :] < member_ids[None, :, None]).astype(ints), axis=2)
    lead = skipped(start, group_id)
    flat_tiles = tiles.reshape(2 * owned, size, size)
    landed = []
    for m in range(2):
        for low, count in parts:
            source = (lead[m][:, None] + low + jnp.arange(count, dtype=ints)[None, :]) * groups
            source = jnp.minimum(source + group_id, owned - 1) + m * owned
            picked = jnp.take(flat_tiles, source.reshape(-1), axis=0, mode="clip")
            landed.append(exchange(picked))

    blocks = jnp.transpose(tokens.reshape(tok_rows, local_blocks, size), (1, 0, 2))
    tok = lax.all_gather(blocks, "mp", axis=0, tiled=True)
    tokt = jnp.transpose(tok, (0, 2, 1))

    first = jnp.sum((holder_all < myself).astype(ints), axis=2)[:, :, None]
    owner_tile = tile_ids[None, None, :]
    q_all = owner_tile // groups - skipped(first, owner_tile % groups)
    slot_all = place(piece_of(owner_tile), member_ids[None, :, None], q_all).reshape(2, -1)
    local_cols = tile_cols - myself * panels
    mask = local_cols[:, None, :] == jnp.arange(panels, dtype=ints)[None, :, None]
    listed = jnp.arange(tile_cols.shape[1])
    before = (listed[:, None] < listed[None, :]).astype(jnp.bfloat16)
    rank = jnp.einsum(
        "mpk,kl->mpl", mask.astype(jnp.bfloat16), before, preferred_element_type=jnp.float32
    ).astype(ints)
    chosen = mask[:, :, None, :] & (
        rank[:, :, None, :] == jnp.arange(KHEAVY, dtype=ints)[None, None, :, None]
    )
    slots = jnp.sum(jnp.where(chosen, slot_all[:, None, None, :], 0), axis=3).reshape(2, -1)
    rows = jnp.sum(jnp.where(chosen, tile_rows[:, None, None, :], 0), axis=3).reshape(2, -1)
    steps = jnp.sum(mask[:, 0, :].astype(ints), axis=1) // KLIGHT

    landed[-1], tok, tokt, slots, rows, steps = lax.optimization_barrier(
        (landed[-1], tok, tokt, slots, rows, steps)
    )
    per_matrix = len(parts)
    arrived = [
        sum([spread(x) for x in landed[m * per_matrix : (m + 1) * per_matrix]], [])
        for m in range(2)
    ]
    piece_count = per_matrix * groups

    slot_bytes = slot_count * size * size * 2
    flops = 2 * panels * KHEAVY * size**2 * tok_rows
    tile_buf = pltpu.VMEM((slot_count, size, size), jnp.bfloat16)
    piece_sems = pltpu.SemaphoreType.DMA((piece_count,))
    params = pltpu.CompilerParams(vmem_limit_bytes=VMEM_BYTES)

    def project(m):
        return pl.pallas_call(
            forward_kernel,
            out_shape=jax.ShapeDtypeStruct(cotangent.shape, jnp.float32),
            in_specs=[smem, smem, smem, vmem] + [anywhere] * piece_count,
            out_specs=vmem,
            scratch_shapes=[tile_buf, piece_sems],
            compiler_params=params,
            cost_estimate=pl.CostEstimate(
                flops=flops, bytes_accessed=4 * slot_bytes, transcendentals=0
            ),
            name="project",
        )(slots[m], rows[m], steps[m : m + 1], tok, *arrived[m])

    gate_pre, up_pre = project(0), project(1)
    sigmoid_gate = jax.nn.sigmoid(gate_pre)
    hidden = (gate_pre * sigmoid_gate * up_pre).astype(jnp.bfloat16)
    upstream = cotangent.astype(jnp.float32)
    gate_grad = (upstream * up_pre * sigmoid_gate * (1.0 + gate_pre * (1.0 - sigmoid_gate))).astype(
        jnp.bfloat16
    )
    up_grad = (upstream * gate_pre * sigmoid_gate).astype(jnp.bfloat16)

    terms_shape = (row_blocks, tok_rows, size)

    def pull_back(m, grad, prior):
        begin = not prior
        piece_shapes = [jax.ShapeDtypeStruct(x.shape, jnp.bfloat16) for x in arrived[m]]
        terms_type = jnp.float32 if begin else jnp.bfloat16
        scratch = [tile_buf, tile_buf, piece_sems]
        results = pl.pallas_call(
            functools.partial(backward_kernel, begin, piece_count),
            out_shape=[jax.ShapeDtypeStruct(terms_shape, terms_type)] + piece_shapes,
            in_specs=[smem, smem, smem] + [vmem] * (2 + len(prior)) + [anywhere] * piece_count,
            out_specs=[vmem] + [anywhere] * piece_count,
            scratch_shapes=scratch if begin else scratch + [pltpu.VMEM(terms_shape, jnp.float32)],
            compiler_params=params,
            cost_estimate=pl.CostEstimate(
                flops=2 * flops, bytes_accessed=6 * slot_bytes, transcendentals=0
            ),
            name="pull_back",
        )(slots[m], rows[m], steps[m : m + 1], tokt, grad, *prior, *arrived[m])
        return results[0], results[1:]

    def add_pair(x, y):
        return x.astype(jnp.float32) + y.astype(jnp.float32)

    def total_of(pieces):
        pair = [
            add_pair(pieces[s], swap_cores(pieces[lanes + s])).astype(jnp.bfloat16)
            for s in range(lanes)
        ]
        total = pair[0].astype(jnp.float32)
        for s in range(1, lanes):
            total = total + shift_y(pair[s], lanes - s).astype(jnp.float32)
        return exchange(total.astype(jnp.bfloat16))

    def totals_of(pieces):
        return [total_of(pieces[i * groups : (i + 1) * groups]) for i in range(per_matrix)]

    def pack(m, returned):
        held = jnp.minimum(jnp.arange(packed, dtype=ints) * groups + group_id, owned - 1)
        holder = jnp.take(my_holder[m], held, mode="clip")
        q = held // groups - jnp.take(lead[m], holder, mode="clip")
        found, base = 0, 0
        for low, count in parts:
            found = jnp.where(q >= low, base + holder * count + q - low, found)
            base += members * count
        return jnp.take(jnp.concatenate(returned, axis=0), found, axis=0, mode="clip")

    gate_terms, gate_pieces = pull_back(0, gate_grad, [])
    terms, up_pieces = pull_back(1, up_grad, [gate_terms])
    gate_back = pack(0, totals_of(gate_pieces))
    up_back = pack(1, totals_of(up_pieces))
    mine = lax.psum_scatter(terms, "mp", scatter_dimension=0, tiled=True)
    up_back, mine = lax.optimization_barrier((up_back, mine))
    home_pieces = spread(gate_back) + spread(up_back)
    input_grad = jnp.transpose(mine, (1, 0, 2)).reshape(tokens.shape)

    home = piece_of(tile_ids) * packed + tile_ids // groups
    chunk = max(c for c in range(1, 29) if owned % c == 0)
    tile_grads = pl.pallas_call(
        collect_kernel,
        out_shape=jax.ShapeDtypeStruct(tiles.shape, jnp.float32),
        grid=(2, owned // chunk),
        in_specs=[smem] + [anywhere] * (2 * groups),
        out_specs=pl.BlockSpec((1, chunk, size, size), lambda m, c: (m, c, 0, 0)),
        scratch_shapes=[
            pltpu.VMEM((groups * packed, size, size), jnp.bfloat16),
            pltpu.SemaphoreType.DMA((groups,)),
        ],
        compiler_params=params,
        name="collect",
    )(jnp.concatenate([home, home]), *home_pieces)
    return (hidden, input_grad, tile_grads)


def solution(mesh):
    in_specs = (P("dp", "mp"), P("dp", "mp"), P(None, "mp", None, None), P(), P())
    out_specs = (P("dp", "mp"), P("dp", "mp"), P(None, "mp", None, None))
    return jax.shard_map(
        per_device, mesh=mesh, in_specs=in_specs, out_specs=out_specs, check_vma=False
    )
```

```python
import functools

import jax
import jax.numpy as jnp
from jax import lax
from jax.experimental import pallas as pl
from jax.experimental.pallas import tpu as pltpu
from jax.sharding import PartitionSpec as P

KHEAVY = 12
KLIGHT = 4
CORES = 2
VMEM_BYTES = 50 * 1024 * 1024


def load_pieces(pieces, buf, sems):
    offset = 0
    copies = []
    for i, piece in enumerate(pieces):
        count = piece.shape[0]
        copies.append(pltpu.make_async_copy(piece, buf.at[pl.ds(offset, count)], sems.at[i]))
        offset += count
    for copy in copies:
        copy.start()
    for copy in copies:
        copy.wait()


def forward_kernel(slots, rows, steps, tok_ref, *refs):
    pieces, (pre_ref, buf, sems) = refs[:-3], refs[-3:]
    load_pieces(pieces, buf, sems)
    size = tok_ref.shape[-1]
    panels = pre_ref.shape[1] // size

    def panel_step(p, carry):
        def group(t, total):
            base = p * KHEAVY + t * KLIGHT
            left = jnp.concatenate([tok_ref[rows[base + i]] for i in range(KLIGHT)], axis=1)
            right = jnp.concatenate([buf[slots[base + i]] for i in range(KLIGHT)], axis=0)
            return total + jnp.dot(left, right, preferred_element_type=jnp.float32)

        total = lax.fori_loop(0, steps[0], group, jnp.zeros((tok_ref.shape[1], size), jnp.float32))
        pre_ref[:, pl.ds(pl.multiple_of(p * size, size), size)] = total
        return carry

    lax.fori_loop(0, panels, panel_step, 0)


def backward_kernel(first, count, out_count, slots, targets, rows, steps, tokt_ref, grad_ref, *refs):
    prior = () if first else refs[:1]
    refs = refs[len(prior) :]
    pieces, terms_out, refs = refs[:count], refs[count], refs[count + 1 :]
    outs, (buf, grads, sems) = refs[:out_count], refs[out_count : out_count + 3]
    terms_ref = terms_out if first else refs[-1]
    load_pieces(pieces, buf, sems)
    size = tokt_ref.shape[1]
    panels = grad_ref.shape[1] // size
    terms_ref[...] = jnp.zeros_like(terms_ref) if first else prior[0][...]

    def panel_step(p, carry):
        column = grad_ref[:, pl.ds(pl.multiple_of(p * size, size), size)]

        def group(t, inner):
            base = p * KHEAVY + t * KLIGHT
            row = [rows[base + i] for i in range(KLIGHT)]
            slot = [slots[base + i] for i in range(KLIGHT)]
            target = [targets[base + i] for i in range(KLIGHT)]
            weight = jnp.concatenate([buf[s] for s in slot], axis=0)
            back = lax.dot_general(
                column, weight, (((1,), (1,)), ((), ())), preferred_element_type=jnp.float32
            )
            picked = jnp.concatenate([tokt_ref[r] for r in row], axis=0)
            outer = jnp.dot(picked, column, preferred_element_type=jnp.float32).astype(grads.dtype)
            before = [terms_ref[r] for r in row]
            for i in range(KLIGHT):
                terms_ref[row[i]] = before[i] + back[:, i * size : (i + 1) * size]
                grads[target[i]] = outer[i * size : (i + 1) * size]
            return inner

        return lax.fori_loop(0, steps[0], group, carry)

    lax.fori_loop(0, panels, panel_step, 0)
    offset = 0
    copies = []
    for i, out in enumerate(outs):
        copies.append(
            pltpu.make_async_copy(grads.at[pl.ds(offset, out.shape[0])], out, sems.at[i])
        )
        offset += out.shape[0]
    for copy in copies:
        copy.start()
    if not first:
        terms_out[...] = terms_ref[...].astype(terms_out.dtype)
    for copy in copies:
        copy.wait()


def collect_kernel(slots, *refs):
    pieces, (out_ref, buf, sems) = refs[:-3], refs[-3:]
    m, c = pl.program_id(0), pl.program_id(1)
    each = len(pieces) // 2

    @pl.when((m == 0) & (c == 0))
    def _():
        load_pieces(pieces[:each], buf, sems)

    @pl.when((m == 1) & (c == 0))
    def _():
        load_pieces(pieces[each:], buf, sems)

    chunk = out_ref.shape[1]
    owned = chunk * pl.num_programs(1)

    def step(i, carry):
        out_ref[0, i] = buf[slots[m * owned + c * chunk + i]].astype(jnp.float32)
        return carry

    lax.fori_loop(0, chunk, step, 0, unroll=True)


def per_device(tokens, cotangent, tiles, tile_rows, tile_cols):
    members = lax.axis_size("mp")
    myself = lax.axis_index("mp")
    groups = lax.axis_size("dp")
    group_id = lax.axis_index("dp")
    lanes = groups // CORES
    my_y, my_core = group_id // CORES, group_id % CORES
    size = tiles.shape[-1]
    owned = tiles.shape[1]
    tok_rows = tokens.shape[0]
    local_blocks = tokens.shape[1] // size
    row_blocks = local_blocks * members
    panels = cotangent.shape[1] // size
    capacity = (panels * KHEAVY + members - 1) // members
    share = (capacity + groups - 1) // groups
    parts = [(0, (share + 1) // 2), ((share + 1) // 2, share // 2)]
    parts = [(low, count) for low, count in parts if count]
    undivided = [(0, share)]
    packed = (owned + groups - 1) // groups
    slot_count = groups * members * share
    smem = pl.BlockSpec(memory_space=pltpu.SMEM)
    vmem = pl.BlockSpec(memory_space=pltpu.VMEM)
    anywhere = pl.BlockSpec(memory_space=pl.ANY)
    ints = jnp.int32

    def piece_of(tile):
        sender = tile % groups
        core_off = (sender % CORES + my_core) % CORES
        y_off = (my_y - sender // CORES + lanes) % lanes
        return core_off * lanes + y_off

    def skipped(start, sender):
        return (start - sender + groups - 1) // groups

    def place(piece, partner, q, cuts):
        found, base = 0, 0
        for low, count in cuts:
            here = base + (piece * members + partner) * count + q - low
            found = jnp.where(q >= low, here, found)
            base += groups * members * count
        return found

    def swap_cores(x):
        pairs = [(d, d - 1 if d % CORES else d + 1) for d in range(groups)]
        return lax.ppermute(x, "dp", pairs)

    def shift_y(x, by):
        pairs = [
            (d, ((d // CORES + by) % lanes) * CORES + d % CORES) for d in range(groups)
        ]
        return lax.ppermute(x, "dp", pairs)

    def both(mine):
        return mine + [swap_cores(piece) for piece in mine]

    def spread(x):
        return both([x] + [shift_y(x, s) for s in range(1, lanes)])

    def exchange(x):
        swapped = lax.all_to_all(
            x.reshape(members, -1, size, size), "mp", split_axis=0, concat_axis=0, tiled=True
        )
        return swapped.reshape(-1, size, size)

    cols_all = tile_cols.reshape(2, members, owned)
    holder_all = cols_all // panels
    my_holder = lax.dynamic_index_in_dim(holder_all, myself, 1, keepdims=False)
    member_ids = jnp.arange(members, dtype=ints)
    tile_ids = jnp.arange(owned, dtype=ints)
    start = jnp.sum((my_holder[:, None, :] < member_ids[None, :, None]).astype(ints), axis=2)
    lead = skipped(start, group_id)
    flat_tiles = tiles.reshape(2 * owned, size, size)
    blocks = jnp.transpose(tokens.reshape(tok_rows, local_blocks, size), (1, 0, 2))
    tok = lax.all_gather(blocks, "mp", axis=0, tiled=True)
    tokt = jnp.transpose(tok, (0, 2, 1))

    first = jnp.sum((holder_all < myself).astype(ints), axis=2)[:, :, None]
    owner_tile = tile_ids[None, None, :]
    q_all = owner_tile // groups - skipped(first, owner_tile % groups)
    slot_all, target_all = [
        place(piece_of(owner_tile), member_ids[None, :, None], q_all, cuts).reshape(2, -1)
        for cuts in (parts, undivided)
    ]
    local_cols = tile_cols - myself * panels
    mask = local_cols[:, None, :] == jnp.arange(panels, dtype=ints)[None, :, None]
    listed = jnp.arange(tile_cols.shape[1])
    before = (listed[:, None] < listed[None, :]).astype(jnp.bfloat16)
    rank = jnp.einsum(
        "mpk,kl->mpl", mask.astype(jnp.bfloat16), before, preferred_element_type=jnp.float32
    ).astype(ints)
    chosen = mask[:, :, None, :] & (
        rank[:, :, None, :] == jnp.arange(KHEAVY, dtype=ints)[None, None, :, None]
    )
    slots = jnp.sum(jnp.where(chosen, slot_all[:, None, None, :], 0), axis=3).reshape(2, -1)
    targets = jnp.sum(jnp.where(chosen, target_all[:, None, None, :], 0), axis=3).reshape(2, -1)
    rows = jnp.sum(jnp.where(chosen, tile_rows[:, None, None, :], 0), axis=3).reshape(2, -1)
    steps = jnp.sum(mask[:, 0, :].astype(ints), axis=1) // KLIGHT

    per_matrix = len(parts)
    piece_count = per_matrix * groups
    slot_bytes = slot_count * size * size * 2
    flops = 2 * panels * KHEAVY * size**2 * tok_rows
    tile_buf = pltpu.VMEM((slot_count, size, size), jnp.bfloat16)
    piece_sems = pltpu.SemaphoreType.DMA((piece_count,))
    params = pltpu.CompilerParams(vmem_limit_bytes=VMEM_BYTES)

    def send(m, low, count, after):
        source = (lead[m][:, None] + low + jnp.arange(count, dtype=ints)[None, :]) * groups
        source = jnp.minimum(source + group_id, owned - 1) + m * owned
        picked = jnp.take(flat_tiles, source.reshape(-1), axis=0, mode="clip")
        picked, after = lax.optimization_barrier((picked, after))
        return exchange(picked), after

    def project(m):
        return pl.pallas_call(
            forward_kernel,
            out_shape=jax.ShapeDtypeStruct(cotangent.shape, jnp.float32),
            in_specs=[smem, smem, smem, vmem] + [anywhere] * piece_count,
            out_specs=vmem,
            scratch_shapes=[tile_buf, piece_sems],
            compiler_params=params,
            cost_estimate=pl.CostEstimate(
                flops=flops, bytes_accessed=4 * slot_bytes, transcendentals=0
            ),
            name="project",
        )(slots[m], rows[m], steps[m : m + 1], tok, *arrived[m])

    stages = [(m, low, count) for m in range(2) for low, count in parts]
    shifted = []
    for i, stage in enumerate(stages):
        last = i == len(stages) - 1
        ready = shifted[i - 2] if i >= 2 else []
        tables = (tok, tokt, slots, targets, rows, steps) if last else ()
        landed, (ready, tables) = send(*stage, (ready, tables))
        if i >= 2:
            shifted[i - 2] = ready
        if last:
            tok, tokt, slots, targets, rows, steps = tables
            arrived = [sum([both(x) for x in shifted[:per_matrix]], [])]
            gate_pre = project(0)
            landed, gate_pre = lax.optimization_barrier((landed, gate_pre))
        shifted.append([landed] + [shift_y(landed, s) for s in range(1, lanes)])
    arrived.append(sum([both(x) for x in shifted[per_matrix:]], []))
    up_pre = project(1)
    sigmoid_gate = jax.nn.sigmoid(gate_pre)
    hidden = (gate_pre * sigmoid_gate * up_pre).astype(jnp.bfloat16)
    upstream = cotangent.astype(jnp.float32)
    gate_grad = (upstream * up_pre * sigmoid_gate * (1.0 + gate_pre * (1.0 - sigmoid_gate))).astype(
        jnp.bfloat16
    )
    up_grad = (upstream * gate_pre * sigmoid_gate).astype(jnp.bfloat16)

    terms_shape = (row_blocks, tok_rows, size)

    def pull_back(m, grad, prior):
        begin = not prior
        piece_shape = jax.ShapeDtypeStruct((members * share, size, size), jnp.bfloat16)
        terms_type = jnp.float32 if begin else jnp.bfloat16
        scratch = [tile_buf, tile_buf, piece_sems]
        results = pl.pallas_call(
            functools.partial(backward_kernel, begin, piece_count, groups),
            out_shape=[jax.ShapeDtypeStruct(terms_shape, terms_type)] + [piece_shape] * groups,
            in_specs=[smem] * 4 + [vmem] * (2 + len(prior)) + [anywhere] * piece_count,
            out_specs=[vmem] + [anywhere] * groups,
            scratch_shapes=scratch if begin else scratch + [pltpu.VMEM(terms_shape, jnp.float32)],
            compiler_params=params,
            cost_estimate=pl.CostEstimate(
                flops=2 * flops, bytes_accessed=6 * slot_bytes, transcendentals=0
            ),
            name="pull_back",
        )(slots[m], targets[m], rows[m], steps[m : m + 1], tokt, grad, *prior, *arrived[m])
        return results[0], results[1:]

    def add_pair(x, y):
        return x.astype(jnp.float32) + y.astype(jnp.float32)

    def pairs_of(pieces):
        return [
            add_pair(pieces[s], swap_cores(pieces[lanes + s])).astype(jnp.bfloat16)
            for s in range(1, lanes)
        ]

    def total_of(pieces, pairs):
        total = add_pair(pieces[0], swap_cores(pieces[lanes]))
        for s in range(1, lanes):
            total = total + shift_y(pairs[s - 1], lanes - s).astype(jnp.float32)
        return exchange(total.astype(jnp.bfloat16))

    def pack(m, returned):
        held = jnp.minimum(jnp.arange(packed, dtype=ints) * groups + group_id, owned - 1)
        holder = jnp.take(my_holder[m], held, mode="clip")
        q = held // groups - jnp.take(lead[m], holder, mode="clip")
        return jnp.take(returned, holder * share + q, axis=0, mode="clip")

    gate_terms, gate_pieces = pull_back(0, gate_grad, [])
    gate_pairs = pairs_of(gate_pieces)
    up_grad, gate_pairs = lax.optimization_barrier((up_grad, gate_pairs))
    terms, up_pieces = pull_back(1, up_grad, [gate_terms])
    gate_back = pack(0, total_of(gate_pieces, gate_pairs))
    up_back = pack(1, total_of(up_pieces, pairs_of(up_pieces)))
    mine = lax.psum_scatter(terms, "mp", scatter_dimension=0, tiled=True)
    up_back, mine = lax.optimization_barrier((up_back, mine))
    home_pieces = spread(gate_back) + spread(up_back)
    input_grad = jnp.transpose(mine, (1, 0, 2)).reshape(tokens.shape)

    home = piece_of(tile_ids) * packed + tile_ids // groups
    chunk = max(c for c in range(1, 29) if owned % c == 0)
    tile_grads = pl.pallas_call(
        collect_kernel,
        out_shape=jax.ShapeDtypeStruct(tiles.shape, jnp.float32),
        grid=(2, owned // chunk),
        in_specs=[smem] + [anywhere] * (2 * groups),
        out_specs=pl.BlockSpec((1, chunk, size, size), lambda m, c: (m, c, 0, 0)),
        scratch_shapes=[
            pltpu.VMEM((groups * packed, size, size), jnp.bfloat16),
            pltpu.SemaphoreType.DMA((groups,)),
        ],
        compiler_params=params,
        name="collect",
    )(jnp.concatenate([home, home]), *home_pieces)
    return (hidden, input_grad, tile_grads)


def solution(mesh):
    in_specs = (P("dp", "mp"), P("dp", "mp"), P(None, "mp", None, None), P(), P())
    out_specs = (P("dp", "mp"), P("dp", "mp"), P(None, "mp", None, None))
    return jax.shard_map(
        per_device, mesh=mesh, in_specs=in_specs, out_specs=out_specs, check_vma=False
    )
```

```python
import functools

import jax
import jax.numpy as jnp
from jax import lax
from jax.experimental import pallas as pl
from jax.experimental.pallas import tpu as pltpu
from jax.sharding import PartitionSpec as P

KHEAVY = 12
KLIGHT = 4
CORES = 2
VMEM_BYTES = 50 * 1024 * 1024


def load_pieces(pieces, buf, sems):
    offset = 0
    copies = []
    for i, piece in enumerate(pieces):
        count = piece.shape[0]
        copies.append(pltpu.make_async_copy(piece, buf.at[pl.ds(offset, count)], sems.at[i]))
        offset += count
    for copy in copies:
        copy.start()
    for copy in copies:
        copy.wait()


def forward_kernel(slots, rows, steps, tok_ref, *refs):
    pieces, (pre_ref, buf, sems) = refs[:-3], refs[-3:]
    load_pieces(pieces, buf, sems)
    size = tok_ref.shape[-1]
    panels = pre_ref.shape[1] // size

    def panel_step(p, carry):
        def group(t, total):
            base = p * KHEAVY + t * KLIGHT
            left = jnp.concatenate([tok_ref[rows[base + i]] for i in range(KLIGHT)], axis=1)
            right = jnp.concatenate([buf[slots[base + i]] for i in range(KLIGHT)], axis=0)
            return total + jnp.dot(left, right, preferred_element_type=jnp.float32)

        total = lax.fori_loop(0, steps[0], group, jnp.zeros((tok_ref.shape[1], size), jnp.float32))
        pre_ref[:, pl.ds(pl.multiple_of(p * size, size), size)] = total
        return carry

    lax.fori_loop(0, panels, panel_step, 0)


def backward_kernel(first, count, out_count, slots, targets, rows, steps, tokt_ref, grad_ref, *refs):
    prior = () if first else refs[:1]
    refs = refs[len(prior) :]
    pieces, terms_out, refs = refs[:count], refs[count], refs[count + 1 :]
    outs, (buf, grads, sems) = refs[:out_count], refs[out_count : out_count + 3]
    terms_ref = terms_out if first else refs[-1]
    load_pieces(pieces, buf, sems)
    size = tokt_ref.shape[1]
    panels = grad_ref.shape[1] // size
    terms_ref[...] = jnp.zeros_like(terms_ref) if first else prior[0][...]

    def panel_step(p, carry):
        column = grad_ref[:, pl.ds(pl.multiple_of(p * size, size), size)]

        def group(t, inner):
            base = p * KHEAVY + t * KLIGHT
            row = [rows[base + i] for i in range(KLIGHT)]
            slot = [slots[base + i] for i in range(KLIGHT)]
            target = [targets[base + i] for i in range(KLIGHT)]
            weight = jnp.concatenate([buf[s] for s in slot], axis=0)
            back = lax.dot_general(
                column, weight, (((1,), (1,)), ((), ())), preferred_element_type=jnp.float32
            )
            picked = jnp.concatenate([tokt_ref[r] for r in row], axis=0)
            outer = jnp.dot(picked, column, preferred_element_type=jnp.float32).astype(grads.dtype)
            before = [terms_ref[r] for r in row]
            for i in range(KLIGHT):
                terms_ref[row[i]] = before[i] + back[:, i * size : (i + 1) * size]
                grads[target[i]] = outer[i * size : (i + 1) * size]
            return inner

        return lax.fori_loop(0, steps[0], group, carry)

    lax.fori_loop(0, panels, panel_step, 0)
    offset = 0
    copies = []
    for i, out in enumerate(outs):
        copies.append(
            pltpu.make_async_copy(grads.at[pl.ds(offset, out.shape[0])], out, sems.at[i])
        )
        offset += out.shape[0]
    for copy in copies:
        copy.start()
    if not first:
        terms_out[...] = terms_ref[...].astype(terms_out.dtype)
    for copy in copies:
        copy.wait()


def collect_kernel(slots, *refs):
    pieces, (out_ref, buf, sems) = refs[:-3], refs[-3:]
    m, c = pl.program_id(0), pl.program_id(1)
    each = len(pieces) // 2

    @pl.when((m == 0) & (c == 0))
    def _():
        load_pieces(pieces[:each], buf, sems)

    @pl.when((m == 1) & (c == 0))
    def _():
        load_pieces(pieces[each:], buf, sems)

    chunk = out_ref.shape[1]
    owned = chunk * pl.num_programs(1)

    def step(i, carry):
        out_ref[0, i] = buf[slots[m * owned + c * chunk + i]].astype(jnp.float32)
        return carry

    lax.fori_loop(0, chunk, step, 0, unroll=True)


def per_device(tokens, cotangent, tiles, tile_rows, tile_cols):
    members = lax.axis_size("mp")
    myself = lax.axis_index("mp")
    groups = lax.axis_size("dp")
    group_id = lax.axis_index("dp")
    lanes = groups // CORES
    my_y, my_core = group_id // CORES, group_id % CORES
    size = tiles.shape[-1]
    owned = tiles.shape[1]
    tok_rows = tokens.shape[0]
    local_blocks = tokens.shape[1] // size
    row_blocks = local_blocks * members
    panels = cotangent.shape[1] // size
    capacity = (panels * KHEAVY + members - 1) // members
    share = (capacity + groups - 1) // groups
    parts = [(0, (share + 1) // 2), ((share + 1) // 2, share // 2)]
    parts = [(low, count) for low, count in parts if count]
    undivided = [(0, share)]
    packed = (owned + groups - 1) // groups
    slot_count = groups * members * share
    smem = pl.BlockSpec(memory_space=pltpu.SMEM)
    vmem = pl.BlockSpec(memory_space=pltpu.VMEM)
    anywhere = pl.BlockSpec(memory_space=pl.ANY)
    ints = jnp.int32

    def piece_of(tile):
        sender = tile % groups
        core_off = (sender % CORES + my_core) % CORES
        y_off = (my_y - sender // CORES + lanes) % lanes
        return core_off * lanes + y_off

    def skipped(start, sender):
        return (start - sender + groups - 1) // groups

    def place(piece, partner, q, cuts):
        found, base = 0, 0
        for low, count in cuts:
            here = base + (piece * members + partner) * count + q - low
            found = jnp.where(q >= low, here, found)
            base += groups * members * count
        return found

    def swap_cores(x):
        pairs = [(d, d - 1 if d % CORES else d + 1) for d in range(groups)]
        return lax.ppermute(x, "dp", pairs)

    def shift_y(x, by):
        pairs = [
            (d, ((d // CORES + by) % lanes) * CORES + d % CORES) for d in range(groups)
        ]
        return lax.ppermute(x, "dp", pairs)

    def both(mine):
        return mine + [swap_cores(piece) for piece in mine]

    def spread(x):
        return both([x] + [shift_y(x, s) for s in range(1, lanes)])

    def exchange(x):
        swapped = lax.all_to_all(
            x.reshape(members, -1, size, size), "mp", split_axis=0, concat_axis=0, tiled=True
        )
        return swapped.reshape(-1, size, size)

    cols_all = tile_cols.reshape(2, members, owned)
    holder_all = cols_all // panels
    my_holder = lax.dynamic_index_in_dim(holder_all, myself, 1, keepdims=False)
    member_ids = jnp.arange(members, dtype=ints)
    tile_ids = jnp.arange(owned, dtype=ints)
    start = jnp.sum((my_holder[:, None, :] < member_ids[None, :, None]).astype(ints), axis=2)
    lead = skipped(start, group_id)
    flat_tiles = tiles.reshape(2 * owned, size, size)
    blocks = jnp.transpose(tokens.reshape(tok_rows, local_blocks, size), (1, 0, 2))
    tok = lax.all_gather(blocks, "mp", axis=0, tiled=True)
    tokt = jnp.transpose(tok, (0, 2, 1))

    first = jnp.sum((holder_all < myself).astype(ints), axis=2)[:, :, None]
    owner_tile = tile_ids[None, None, :]
    q_all = owner_tile // groups - skipped(first, owner_tile % groups)
    slot_all, target_all = [
        place(piece_of(owner_tile), member_ids[None, :, None], q_all, cuts).reshape(2, -1)
        for cuts in (parts, undivided)
    ]
    local_cols = tile_cols - myself * panels
    mask = local_cols[:, None, :] == jnp.arange(panels, dtype=ints)[None, :, None]
    listed = jnp.arange(tile_cols.shape[1])
    before = (listed[:, None] < listed[None, :]).astype(jnp.bfloat16)
    rank = jnp.einsum(
        "mpk,kl->mpl", mask.astype(jnp.bfloat16), before, preferred_element_type=jnp.float32
    ).astype(ints)
    chosen = mask[:, :, None, :] & (
        rank[:, :, None, :] == jnp.arange(KHEAVY, dtype=ints)[None, None, :, None]
    )
    slots = jnp.sum(jnp.where(chosen, slot_all[:, None, None, :], 0), axis=3).reshape(2, -1)
    targets = jnp.sum(jnp.where(chosen, target_all[:, None, None, :], 0), axis=3).reshape(2, -1)
    rows = jnp.sum(jnp.where(chosen, tile_rows[:, None, None, :], 0), axis=3).reshape(2, -1)
    steps = jnp.sum(mask[:, 0, :].astype(ints), axis=1) // KLIGHT

    per_matrix = len(parts)
    piece_count = per_matrix * groups
    slot_bytes = slot_count * size * size * 2
    flops = 2 * panels * KHEAVY * size**2 * tok_rows
    tile_buf = pltpu.VMEM((slot_count, size, size), jnp.bfloat16)
    piece_sems = pltpu.SemaphoreType.DMA((piece_count,))
    params = pltpu.CompilerParams(vmem_limit_bytes=VMEM_BYTES)

    def send(m, low, count, after):
        source = (lead[m][:, None] + low + jnp.arange(count, dtype=ints)[None, :]) * groups
        source = jnp.minimum(source + group_id, owned - 1) + m * owned
        picked = jnp.take(flat_tiles, source.reshape(-1), axis=0, mode="clip")
        picked, after = lax.optimization_barrier((picked, after))
        return exchange(picked), after

    def project(m):
        return pl.pallas_call(
            forward_kernel,
            out_shape=jax.ShapeDtypeStruct(cotangent.shape, jnp.float32),
            in_specs=[smem, smem, smem, vmem] + [anywhere] * piece_count,
            out_specs=vmem,
            scratch_shapes=[tile_buf, piece_sems],
            compiler_params=params,
            cost_estimate=pl.CostEstimate(
                flops=flops, bytes_accessed=4 * slot_bytes, transcendentals=0
            ),
            name="project",
        )(slots[m], rows[m], steps[m : m + 1], tok, *arrived[m])

    stages = [(m, low, count) for m in range(2) for low, count in parts]
    shifted = []
    for i, stage in enumerate(stages):
        last = i == len(stages) - 1
        ready = shifted[i - 2] if i >= 2 else []
        tables = (tok, tokt, slots, targets, rows, steps) if last else ()
        landed, (ready, tables) = send(*stage, (ready, tables))
        if i >= 2:
            shifted[i - 2] = ready
        if last:
            tok, tokt, slots, targets, rows, steps = tables
            arrived = [sum([both(x) for x in shifted[:per_matrix]], [])]
            gate_pre = project(0)
            landed, gate_pre = lax.optimization_barrier((landed, gate_pre))
        shifted.append([landed] + [shift_y(landed, s) for s in range(1, lanes)])
    arrived.append(sum([both(x) for x in shifted[per_matrix:]], []))
    up_pre = project(1)
    sigmoid_gate = jax.nn.sigmoid(gate_pre)
    hidden = (gate_pre * sigmoid_gate * up_pre).astype(jnp.bfloat16)
    upstream = cotangent.astype(jnp.float32)
    gate_grad = (upstream * up_pre * sigmoid_gate * (1.0 + gate_pre * (1.0 - sigmoid_gate))).astype(
        jnp.bfloat16
    )
    up_grad = (upstream * gate_pre * sigmoid_gate).astype(jnp.bfloat16)

    terms_shape = (row_blocks, tok_rows, size)

    def pull_back(m, grad, prior):
        begin = not prior
        piece_shape = jax.ShapeDtypeStruct((members * share, size, size), jnp.bfloat16)
        terms_type = jnp.float32 if begin else jnp.bfloat16
        scratch = [tile_buf, tile_buf, piece_sems]
        results = pl.pallas_call(
            functools.partial(backward_kernel, begin, piece_count, groups),
            out_shape=[jax.ShapeDtypeStruct(terms_shape, terms_type)] + [piece_shape] * groups,
            in_specs=[smem] * 4 + [vmem] * (2 + len(prior)) + [anywhere] * piece_count,
            out_specs=[vmem] + [anywhere] * groups,
            scratch_shapes=scratch if begin else scratch + [pltpu.VMEM(terms_shape, jnp.float32)],
            compiler_params=params,
            cost_estimate=pl.CostEstimate(
                flops=2 * flops, bytes_accessed=6 * slot_bytes, transcendentals=0
            ),
            name="pull_back",
        )(slots[m], targets[m], rows[m], steps[m : m + 1], tokt, grad, *prior, *arrived[m])
        return results[0], results[1:]

    def add_pair(x, y):
        return x.astype(jnp.float32) + y.astype(jnp.float32)

    def pairs_of(pieces):
        return [
            add_pair(pieces[s], swap_cores(pieces[lanes + s])).astype(jnp.bfloat16)
            for s in range(1, lanes)
        ]

    def total_of(pieces, pairs):
        total = add_pair(pieces[0], swap_cores(pieces[lanes]))
        for s in range(1, lanes):
            total = total + shift_y(pairs[s - 1], lanes - s).astype(jnp.float32)
        return exchange(total.astype(jnp.bfloat16))

    def pack(m, returned):
        held = jnp.minimum(jnp.arange(packed, dtype=ints) * groups + group_id, owned - 1)
        holder = jnp.take(my_holder[m], held, mode="clip")
        q = held // groups - jnp.take(lead[m], holder, mode="clip")
        return jnp.take(returned, holder * share + q, axis=0, mode="clip")

    gate_terms, gate_pieces = pull_back(0, gate_grad, [])
    gate_pairs = pairs_of(gate_pieces)
    up_grad, gate_pairs = lax.optimization_barrier((up_grad, gate_pairs))
    terms, up_pieces = pull_back(1, up_grad, [gate_terms])
    gate_back = pack(0, total_of(gate_pieces, gate_pairs))
    up_back = pack(1, total_of(up_pieces, pairs_of(up_pieces)))
    mine = lax.psum_scatter(terms, "mp", scatter_dimension=0, tiled=True)
    home_pieces = spread(gate_back) + spread(up_back)
    home_pieces[-1], mine = lax.optimization_barrier((home_pieces[-1], mine))
    input_grad = jnp.transpose(mine, (1, 0, 2)).reshape(tokens.shape)

    home = piece_of(tile_ids) * packed + tile_ids // groups
    chunk = max(c for c in range(1, 29) if owned % c == 0)
    tile_grads = pl.pallas_call(
        collect_kernel,
        out_shape=jax.ShapeDtypeStruct(tiles.shape, jnp.float32),
        grid=(2, owned // chunk),
        in_specs=[smem] + [anywhere] * (2 * groups),
        out_specs=pl.BlockSpec((1, chunk, size, size), lambda m, c: (m, c, 0, 0)),
        scratch_shapes=[
            pltpu.VMEM((groups * packed, size, size), jnp.bfloat16),
            pltpu.SemaphoreType.DMA((groups,)),
        ],
        compiler_params=params,
        name="collect",
    )(jnp.concatenate([home, home]), *home_pieces)
    return (hidden, input_grad, tile_grads)


def solution(mesh):
    in_specs = (P("dp", "mp"), P("dp", "mp"), P(None, "mp", None, None), P(), P())
    out_specs = (P("dp", "mp"), P("dp", "mp"), P(None, "mp", None, None))
    return jax.shard_map(
        per_device, mesh=mesh, in_specs=in_specs, out_specs=out_specs, check_vma=False
    )
```
